256 devices in a mesh: dp: 32 (over x, z), tensor: 8 (over y, core).
Axes of the slice: x: 4, y: 4, z: 8, core: 2. Of those that a mesh axis runs over, the one named last changes fastest.
Arguments:
- gate_input: bfloat16 [8192, 14336], P('dp', 'tensor'), may hold values from -12 to 12
- up_input: bfloat16 [8192, 14336], P('dp', 'tensor'), may hold values from -12 to 12
- grad_out: bfloat16 [8192, 4096], P('dp'), may hold values from -0.0501 to 0.0501
Outputs:
- combined: bfloat16 [14336, 4096], P('tensor', 'dp')
The draws below stay inside these ranges and needn't reach their ends.
All inputs are finite; a program needn't handle non-finite values.
Results may differ from the reference program's by a relative error of at most 0.0059.
Values may be sent and summed in bfloat16 or wider, within the bound.
A program may use at most 128 MiB of HBM per device.

```python
import math
import jax
import jax.numpy as jnp
from jax import lax

D = 4096
FF = 14336
TOK_DEV = 256
REPLICAS = 32
TOKENS = 8192
LEVELS = 5


def scaled_field(key, own_part, common_part, rise):
    rows_total, cols_total = own_part.shape
    key_rows, key_cols = jax.random.split(key)
    row_scale = jnp.exp(jax.random.uniform(key_rows, (rows_total, 1), jnp.float32, -1.2, 1.2))
    col_scale = jnp.exp(jax.random.uniform(key_cols, (1, cols_total), jnp.float32, -0.7, 0.7))
    tiled = jnp.tile(common_part, (rows_total // common_part.shape[0], 1))
    return (tiled + own_part) * row_scale * col_scale * rise


def saved_field(key, limit):
    key_own, key_common, key_scale = jax.random.split(key, 3)
    own_part = 0.6 * jax.random.normal(key_own, (TOKENS, FF), jnp.float32)
    common_part = 0.8 * jax.random.normal(key_common, (TOK_DEV, FF), jnp.float32)
    growth = math.log(3.0)
    position = jnp.arange(FF, dtype=jnp.float32)[None, :] / (FF - 1)
    rise = jnp.exp(growth * position)
    return jnp.clip(scaled_field(key_scale, own_part, common_part, rise), -limit, limit)


def draw_gate_input(key, part):
    key = jax.random.fold_in(key, 3)
    return saved_field(key, 12.0).astype(jnp.bfloat16)


def draw_up_input(key, part):
    key = jax.random.fold_in(key, 7)
    return saved_field(key, 12.0).astype(jnp.bfloat16)


def draw_grad_out(key, part):
    key = jax.random.fold_in(key, 11)
    key_own, key_common, key_scale = jax.random.split(key, 3)
    own_part = 0.6 * jax.random.normal(key_own, (TOKENS, D), jnp.float32)
    common_part = 0.8 * jax.random.normal(key_common, (TOK_DEV, D), jnp.float32)
    growth = math.log(3.0)
    replica_count = TOKENS // TOK_DEV
    replica_pos = (jnp.arange(TOKENS) // TOK_DEV).astype(jnp.float32)[:, None] / (replica_count - 1)
    rise = jnp.exp(growth * replica_pos)
    raw_field = scaled_field(key_scale, own_part, common_part, rise)
    return (jnp.clip(raw_field, -25.0, 25.0) * 0.002).astype(jnp.bfloat16)


def setup_inputs(seed: int = 0) -> dict:
    streams_of = jax.random.split(jax.random.key(seed), 4)
    return {
        "gate_input": draw_gate_input(jax.random.fold_in(streams_of[3], 71), 0),
        "up_input": draw_up_input(jax.random.fold_in(streams_of[3], 71), 0),
        "grad_out": draw_grad_out(jax.random.fold_in(streams_of[3], 71), 0),
    }


epsilon = 1e-06

def adasum_pair(first_vec, second_vec):
    first_vec = lax.optimization_barrier(first_vec).astype(jnp.float32)
    second_vec = lax.optimization_barrier(second_vec).astype(jnp.float32)
    self_first = jnp.sum(first_vec * first_vec)
    self_second = jnp.sum(second_vec * second_vec)
    cross_term = jnp.sum(first_vec * second_vec)
    coef_first = 1.0 - cross_term / (2.0 * (self_first + epsilon))
    coef_second = 1.0 - cross_term / (2.0 * (self_second + epsilon))
    return (coef_first * first_vec + coef_second * second_vec).astype(jnp.bfloat16)

def reference(gate_input, up_input, grad_out):
    hidden = (jax.nn.silu(gate_input.astype(jnp.float32)) * up_input.astype(jnp.float32)).astype(jnp.bfloat16)

    def leaf_grad(replica):
        rows_hidden = hidden[replica * TOK_DEV:(replica + 1) * TOK_DEV]
        rows_grad = grad_out[replica * TOK_DEV:(replica + 1) * TOK_DEV]
        product = lax.dot_general(rows_hidden, rows_grad, (((0,), (0,)), ((), ())), preferred_element_type=jnp.float32)
        return product.astype(jnp.bfloat16)

    def tree_node(level, index):
        if level == 0:
            return leaf_grad(index)
        stride = REPLICAS >> level
        return adasum_pair(tree_node(level - 1, index), tree_node(level - 1, index + stride))
    return tree_node(LEVELS, 0)
```

```python
import jax
import jax.numpy as jnp
from jax import lax
from jax.experimental import pallas as pl
from jax.experimental.pallas import tpu as pltpu
from jax.sharding import PartitionSpec as P

epsilon = 1e-06
MESH = pl.DeviceIdType.MESH
NX, NZ, NT = 4, 8, 8
TOK = 256
HID = 1792
MB = HID // NZ
NB = 1024
TR = TOK // NT
ORDER = (0, 7, 1, 6, 2, 5, 3, 4)
PAIRS4 = [(i, j) for i in range(4) for j in range(i, 4)]
PAIRS8 = [(i, j) for i in range(8) for j in range(i, 8)]


def pair_coefs(aa, bb, ab):
    aa = jnp.maximum(aa, 0.0)
    bb = jnp.maximum(bb, 0.0)
    bound = jnp.sqrt(aa) * jnp.sqrt(bb)
    ab = jnp.clip(ab, -bound, bound)
    return 1.0 - ab / (2.0 * (aa + epsilon)), 1.0 - ab / (2.0 * (bb + epsilon))


def tree_weights(gram, count):
    def get(table, i, j):
        return table[(min(i, j), max(i, j))]

    weights = [None] * count
    while count > 1:
        half = count // 2
        coefs = [
            pair_coefs(gram[(j, j)], gram[(j + half, j + half)], get(gram, j, j + half))
            for j in range(half)
        ]
        merged = {}
        for i in range(half):
            for j in range(i, half):
                merged[(i, j)] = (
                    coefs[i][0] * coefs[j][0] * get(gram, i, j)
                    + coefs[i][0] * coefs[j][1] * get(gram, i, j + half)
                    + coefs[i][1] * coefs[j][0] * get(gram, i + half, j)
                    + coefs[i][1] * coefs[j][1] * get(gram, i + half, j + half)
                )
        for k in range(len(weights)):
            node = k % count
            factor = coefs[node % half][node // half]
            weights[k] = factor if weights[k] is None else weights[k] * factor
        gram, count = merged, half
    return weights


def kernel(
    gate, up, grad, out,
    hown, hb, gb, leaf, pbuf, wbuf, ar, cst, obuf,
    own_sem, gx_s, gx_r, hz_s, hz_r, gz_s, gz_r, gy_s, gy_r, sib_s, sib_r, hx_s, hx_r, ar_s, ar_r, oz_s, oz_r,
):
    dp = lax.axis_index("dp")
    t = lax.axis_index("tensor")
    x, z = lax.div(dp, NZ), lax.rem(dp, NZ)
    y, core = lax.div(t, 2), lax.rem(t, 2)
    sib = y * 2 + 1 - core

    def xo(k):
        return lax.rem(x + k, NX)

    def zo(k):
        return lax.rem(z + k, NZ)

    def to(k):
        return lax.rem(t + k, NT)

    def yo(k):
        return lax.rem(y + k, 4) * 2 + core

    def at_x(k):
        return (xo(k) * NZ + z, t)

    def at_z(k):
        return (x * NZ + zo(k), t)

    def at_t(rank):
        return (dp, rank)

    def remote(src, dst, send, recv, where):
        return pltpu.make_async_remote_copy(
            src_ref=src, dst_ref=dst, send_sem=send, recv_sem=recv, device_id=where, device_id_type=MESH
        )

    sent = []

    def send(src, dst, ss, rs, where):
        copy = remote(src, dst, ss, rs, where)
        copy.start()
        sent.append(copy)

    def arrived(dst, ss, rs):
        remote(dst, dst, ss, rs, at_x(1)).wait_recv()

    def gpart(zc, rank, lo=0, n=NX):
        return gb.at[pl.ds(lo, n), zc, pl.ds(pl.multiple_of(rank * TR, TR), TR), :]

    barrier = pltpu.get_barrier_semaphore()
    partners = [at_x(k) for k in range(1, NX)] + [at_z(k) for k in range(1, NZ)] + [at_t(to(k)) for k in range(1, NT)]
    for where in partners:
        pl.semaphore_signal(barrier, inc=1, device_id=where, device_id_type=MESH)
    pl.semaphore_wait(barrier, len(partners))

    rows_t = pl.ds(pl.multiple_of(t * TR, TR), TR)
    for k in range(1, NX):
        cols = pl.ds(pl.multiple_of(xo(k) * NB, NB), NB)
        send(grad.at[rows_t, cols], gb.at[x, z, rows_t, :], gx_s.at[k], gx_r.at[k], at_x(k))
    own_g = pltpu.make_async_copy(
        grad.at[rows_t, pl.ds(pl.multiple_of(x * NB, NB), NB)], gb.at[x, z, rows_t, :], own_sem.at[0]
    )
    own_g.start()

    for j in range(HID // 128):
        cols = slice(128 * j, 128 * j + 128)
        v = gate[:, cols].astype(jnp.float32)
        u = up[:, cols].astype(jnp.float32)
        h = v / (1.0 + jnp.exp(-v)) * u
        hown[cols, :] = h.T.astype(jnp.bfloat16)

    def hown_at(zc):
        return hown.at[pl.ds(pl.multiple_of(zc * MB, 16), MB), :]

    own_h = pltpu.make_async_copy(hown_at(z), hb.at[x, z], own_sem.at[1])
    own_h.start()

    def start_hz(k):
        send(hown_at(zo(k)), hb.at[x, z], hz_s.at[k], hz_r.at[k], at_z(k))

    def g_z(i):
        o = ORDER[i]
        zc = zo(o)
        if o == 0:
            own_g.wait()
            for k in range(1, NX):
                arrived(gb.at[xo(NX - k), z, rows_t, :], gx_s.at[k], gx_r.at[k])
            send(gpart(zc, t), gpart(zc, t), gz_s.at[0, 1], gz_r.at[0, 1], at_z(1))
            send(gpart(zc, t), gpart(zc, t), gz_s.at[1, 1], gz_r.at[1, 1], at_z(7))
        elif o == 4:
            arrived(gpart(zc, t, 0, 2), gz_s.at[0, 4], gz_r.at[0, 4])
            arrived(gpart(zc, t, 2, 2), gz_s.at[1, 4], gz_r.at[1, 4])
        else:
            way, step = (0, 8 - o) if o > 4 else (1, o)
            arrived(gpart(zc, t), gz_s.at[way, step], gz_r.at[way, step])
            part = (0, 4) if step < 3 else (2 * way, 2)
            send(
                gpart(zc, t, *part), gpart(zc, t, *part),
                gz_s.at[way, step + 1], gz_r.at[way, step + 1], at_z(1 if way == 0 else 7),
            )
        send(gpart(zc, t), gpart(zc, t), gy_s.at[0, o], gy_r.at[0, o], at_t(yo(1)))
        send(gpart(zc, t), gpart(zc, t), gy_s.at[1, o], gy_r.at[1, o], at_t(yo(3)))
        send(gpart(zc, t), gpart(zc, t), sib_s.at[0, o], sib_r.at[0, o], at_t(sib))

    def g_y(i):
        o = ORDER[i]
        zc = zo(o)
        for way in range(2):
            rank = yo(3 if way == 0 else 1)
            arrived(gpart(zc, rank), gy_s.at[way, o], gy_r.at[way, o])
            half = gpart(zc, rank, 2 * way, 2)
            send(half, half, gy_s.at[2 + way, o], gy_r.at[2 + way, o], at_t(yo(1 if way == 0 else 3)))
            whole = gpart(zc, rank)
            send(whole, whole, sib_s.at[1 + way, o], sib_r.at[1 + way, o], at_t(sib))

    def g_far(i):
        o = ORDER[i]
        zc = zo(o)
        for way in range(2):
            half = gpart(zc, yo(2), 2 * way, 2)
            arrived(half, gy_s.at[2 + way, o], gy_r.at[2 + way, o])
            send(half, half, sib_s.at[3 + way, o], sib_r.at[3 + way, o], at_t(sib))

    def h_z(i):
        o = ORDER[i]
        zc = zo(o)
        if o == 0:
            own_h.wait()
        else:
            arrived(hb.at[x, zc], hz_s.at[8 - o], hz_r.at[8 - o])
        send(hb.at[x, zc], hb.at[x, zc], hx_s.at[0, o], hx_r.at[0, o], at_x(1))
        send(hb.at[x, zc], hb.at[x, zc], hx_s.at[1, o], hx_r.at[1, o], at_x(3))

    def h_x(i):
        o = ORDER[i]
        zc = zo(o)
        for way in range(2):
            xs = xo(3 if way == 0 else 1)
            arrived(hb.at[xs, zc], hx_s.at[way, o], hx_r.at[way, o])
            half = hb.at[xs, zc, pl.ds(way * (MB // 2), MB // 2), :]
            send(half, half, hx_s.at[2 + way, o], hx_r.at[2 + way, o], at_x(1 if way == 0 else 3))

    def finish(i):
        o = ORDER[i]
        zc = zo(o)
        for way in range(2):
            half = hb.at[xo(2), zc, pl.ds(way * (MB // 2), MB // 2), :]
            arrived(half, hx_s.at[2 + way, o], hx_r.at[2 + way, o])
        other = 1 - 2 * core
        arrived(gpart(zc, sib), sib_s.at[0, o], sib_r.at[0, o])
        arrived(gpart(zc, yo(3) + other), sib_s.at[1, o], sib_r.at[1, o])
        arrived(gpart(zc, yo(1) + other), sib_s.at[2, o], sib_r.at[2, o])
        arrived(gpart(zc, yo(2) + other, 0, 2), sib_s.at[3, o], sib_r.at[3, o])
        arrived(gpart(zc, yo(2) + other, 2, 2), sib_s.at[4, o], sib_r.at[4, o])

        def product(k, _):
            xx = lax.div(k, 4)
            cols = pl.ds(pl.multiple_of(lax.rem(k, 4) * 256, 256), 256)
            leaf[zc, xx, :, cols] = jnp.dot(hb[xx, zc], gb[xx, zc, :, cols], preferred_element_type=jnp.float32)
            return 0

        lax.fori_loop(0, 16, product, 0)

        def gram(k, sums):
            rows = pl.ds(pl.multiple_of(k * 8, 8), 8)
            for c in range(NB // 128):
                vals = [leaf[zc, xx, rows, 128 * c:128 * c + 128] for xx in range(4)]
                sums = tuple(s + vals[a] * vals[b] for s, (a, b) in zip(sums, PAIRS4))
            return sums

        sums = lax.fori_loop(0, MB // 8, gram, (jnp.zeros((8, 128), jnp.float32),) * len(PAIRS4))
        for k, s in enumerate(sums):
            pbuf[0, k * 8 + zc] = s

    def all_sum(which):
        rows = jnp.sum(pbuf[which], axis=1)
        value = jnp.broadcast_to(jnp.sum(rows.T, axis=0, keepdims=True), (8, 128))
        for phase, (count, me) in enumerate(((NT, t), (NX, x), (NZ, z))):
            slots = ar.at[which, phase]
            slots[me] = value
            for k in range(1, count):
                where = (at_t(to(k)), at_x(k), at_z(k))[phase]
                send(slots.at[me], slots.at[me], ar_s.at[which, phase, k], ar_r.at[which, phase, k], where)
            for k in range(1, count):
                arrived(
                    slots.at[lax.rem(me + count - k, count)], ar_s.at[which, phase, k], ar_r.at[which, phase, k]
                )
            value = jnp.sum(slots[0:count], axis=0)
        return jnp.broadcast_to(value[0:1], (128, 128)).T

    pbuf[...] = jnp.zeros_like(pbuf)
    stages = ((g_z, 0), (g_y, 1), (g_far, 2), (h_z, 0), (h_x, 1), (finish, 3))
    for k in range(1, 5):
        start_hz(k)
        if k < 4:
            start_hz(8 - k)
    for i in range(NZ + 3):
        for stage, lag in stages:
            if 0 <= i - lag < NZ:
                stage(i - lag)

    table = all_sum(0)
    weights = tree_weights({pair: table[8 * k:8 * k + 8] for k, pair in enumerate(PAIRS4)}, 4)
    for zz in range(NZ):
        for xx in range(NX):
            wbuf[zz * 4 + xx] = jnp.broadcast_to(weights[xx][zz:zz + 1], (8, 128))

    def merge(k, sums):
        rows = pl.ds(pl.multiple_of(k * 8, 8), 8)
        for c in range(NB // 128):
            cols = slice(128 * c, 128 * c + 128)
            nodes = []
            for zz in range(NZ):
                parts = [wbuf[zz * 4 + xx] * leaf[zz, xx, rows, cols] for xx in range(NX)]
                node = (parts[0] + parts[1]) + (parts[2] + parts[3])
                leaf[zz, 0, rows, cols] = node
                nodes.append(node)
            sums = tuple(s + nodes[a] * nodes[b] for s, (a, b) in zip(sums, PAIRS8))
        return sums

    sums = lax.fori_loop(0, MB // 8, merge, (jnp.zeros((8, 128), jnp.float32),) * len(PAIRS8))
    for k, s in enumerate(sums):
        pbuf[1, k] = s

    table = all_sum(1)
    weights = tree_weights({pair: table[k:k + 1] for k, pair in enumerate(PAIRS8)}, 8)
    for k in (4, 3, 5, 2, 6, 1, 7, 0):
        zt = zo(k)
        cols = pl.ds(pl.multiple_of(zt * 128, 128), 128)
        total = weights[0] * leaf[0, 0, :, cols]
        for zz in range(1, NZ):
            total = total + weights[zz] * leaf[zz, 0, :, cols]
        cst[k] = total.astype(jnp.bfloat16)
        if k:
            send(cst.at[k], obuf.at[z], oz_s.at[k], oz_r.at[k], at_z(k))
    out[pl.ds(pl.multiple_of(z * MB, 16), MB), :] = cst[0]
    for k in range(1, NZ):
        zs = zo(NZ - k)
        arrived(obuf.at[zs], oz_s.at[k], oz_r.at[k])
        out[pl.ds(pl.multiple_of(zs * MB, 16), MB), :] = obuf[zs]
    for copy in sent:
        copy.wait_send()


def body(gate_input, up_input, grad_out):
    dma = pltpu.SemaphoreType.DMA
    vmem = pl.BlockSpec(memory_space=pltpu.VMEM)
    return pl.pallas_call(
        kernel,
        out_shape=jax.ShapeDtypeStruct((HID, 128), jnp.bfloat16),
        in_specs=[vmem, vmem, pl.BlockSpec(memory_space=pl.ANY)],
        out_specs=vmem,
        scratch_shapes=[
            pltpu.VMEM((HID, TOK), jnp.bfloat16),
            pltpu.VMEM((NX, NZ, MB, TOK), jnp.bfloat16),
            pltpu.VMEM((NX, NZ, TOK, NB), jnp.bfloat16),
            pltpu.VMEM((NZ, NX, MB, NB), jnp.float32),
            pltpu.VMEM((2, 128, 8, 128), jnp.float32),
            pltpu.VMEM((NZ * NX, 8, 128), jnp.float32),
            pltpu.VMEM((2, 3, 8, 8, 128), jnp.float32),
            pltpu.VMEM((NZ, MB, 128), jnp.bfloat16),
            pltpu.VMEM((NZ, MB, 128), jnp.bfloat16),
            dma((2,)),
            dma((NX,)), dma((NX,)),
            dma((NZ,)), dma((NZ,)),
            dma((2, 5)), dma((2, 5)),
            dma((4, NZ)), dma((4, NZ)),
            dma((5, NZ)), dma((5, NZ)),
            dma((4, NZ)), dma((4, NZ)),
            dma((2, 3, 8)), dma((2, 3, 8)),
            dma((NZ,)), dma((NZ,)),
        ],
        compiler_params=pltpu.CompilerParams(
            collective_id=0, has_side_effects=True, vmem_limit_bytes=62 * 1024 * 1024
        ),
        cost_estimate=pl.CostEstimate(flops=3_760_000_000, bytes_accessed=5_000_000, transcendentals=460_000),
    )(gate_input, up_input, grad_out)


def solution(mesh):
    placed = (P("dp", "tensor"), P("dp", "tensor"), P("dp", None))
    return jax.shard_map(
        body, mesh=mesh, in_specs=placed, out_specs=P("tensor", "dp"), check_vma=False
    )
```

```python
import functools

import jax
import jax.numpy as jnp
from jax import lax
from jax.experimental import pallas as pl
from jax.experimental.pallas import tpu as pltpu
from jax.sharding import PartitionSpec as P

epsilon = 1e-06
MESH = pl.DeviceIdType.MESH
NX, NZ, NT = 4, 8, 8
TOK = 256
HID = 1792
MB = HID // NZ
NB = 1024
TR = TOK // NT
HR = TOK // 2
CS = 768
ORDER = (0, 7, 1, 6, 2, 5, 3, 4)
SCHEDULE = (
    "h0", "s1", "s7", "s2", "s6", "q0", "r0", "h1", "h2", "x0", "y0", "h3", "h4", "x1", "x2", "f0",
    "q1", "q2", "x3", "x4", "c0", "y1", "r1", "r2", "y2", "f1",
    "q3", "q4", "s3", "s5", "f2", "c1", "y3", "r3", "r4", "c2", "y4", "f3",
    "q5", "q6", "s4", "f4", "h5", "h6", "c3", "x5", "y5", "r5", "r6", "x6", "y6", "c4",
    "q7", "f5", "r7", "f6", "h7", "c5", "y7", "x7", "c6", "f7", "c7",
)
PAIRS4 = [(i, j) for i in range(4) for j in range(i, 4)]
ALL4 = [(i, j) for i in range(4) for j in range(4)]
PAIRS8 = [(i, j) for i in range(8) for j in range(i, 8)]


def pair_coefs(aa, bb, ab):
    aa = jnp.maximum(aa, 0.0)
    bb = jnp.maximum(bb, 0.0)
    bound = jnp.sqrt(aa) * jnp.sqrt(bb)
    ab = jnp.clip(ab, -bound, bound)
    return 1.0 - ab / (2.0 * (aa + epsilon)), 1.0 - ab / (2.0 * (bb + epsilon))


def tree_weights(gram, count):
    def get(table, i, j):
        return table[(min(i, j), max(i, j))]

    weights = [None] * count
    while count > 1:
        half = count // 2
        coefs = [
            pair_coefs(gram[(j, j)], gram[(j + half, j + half)], get(gram, j, j + half))
            for j in range(half)
        ]
        merged = {}
        for i in range(half):
            for j in range(i, half):
                merged[(i, j)] = (
                    coefs[i][0] * coefs[j][0] * get(gram, i, j)
                    + coefs[i][0] * coefs[j][1] * get(gram, i, j + half)
                    + coefs[i][1] * coefs[j][0] * get(gram, i + half, j)
                    + coefs[i][1] * coefs[j][1] * get(gram, i + half, j + half)
                )
        for k in range(len(weights)):
            node = k % count
            factor = coefs[node % half][node // half]
            weights[k] = factor if weights[k] is None else weights[k] * factor
        gram, count = merged, half
    return weights


def kernel(
    gate, up, grad, out,
    hown, hb, gb, leaf, pbuf, wbuf, ar, cst, obuf,
    own_sem, gx_s, gx_r, hz_s, hz_r, gz_s, gz_r, gy_s, gy_r, sib_s, sib_r, hx_s, hx_r, ar_s, ar_r, oz_s, oz_r,
):
    dp = lax.axis_index("dp")
    t = lax.axis_index("tensor")
    x, z = lax.div(dp, NZ), lax.rem(dp, NZ)
    y, core = lax.div(t, 2), lax.rem(t, 2)
    sib = y * 2 + 1 - core

    def xo(k):
        return lax.rem(x + k, NX)

    def zo(k):
        return lax.rem(z + k, NZ)

    def to(k):
        return lax.rem(t + k, NT)

    def yo(k):
        return lax.rem(y + k, 4) * 2 + core

    def at_x(k):
        return (xo(k) * NZ + z, t)

    def at_z(k):
        return (x * NZ + zo(k), t)

    def at_t(rank):
        return (dp, rank)

    def remote(src, dst, send, recv, where):
        return pltpu.make_async_remote_copy(
            src_ref=src, dst_ref=dst, send_sem=send, recv_sem=recv, device_id=where, device_id_type=MESH
        )

    sent, done = [], []

    def send(src, dst, ss, rs, where):
        copy = remote(src, dst, ss, rs, where)
        copy.start()
        sent.append(copy)

    def arrived(dst, ss, rs):
        remote(dst, dst, ss, rs, at_x(1)).wait_recv()

    def quarter(zc, yy, lo=0, n=NX, c=core):
        rows = pl.ds(pl.multiple_of(c * HR + lax.rem(y + yy, 4) * TR, TR), TR)
        return gb.at[pl.ds(lo, n), zc, rows, pl.ds(0, CS)]

    def rest(zc, lo=0, n=NX, c=core):
        return gb.at[pl.ds(lo, n), zc, pl.ds(pl.multiple_of(c * HR, HR), HR), pl.ds(CS, NB - CS)]

    barrier = pltpu.get_barrier_semaphore()
    partners = [at_x(k) for k in range(1, NX)] + [at_z(k) for k in range(1, NZ)] + [at_t(to(k)) for k in range(1, NT)]
    for where in partners:
        pl.semaphore_signal(barrier, inc=1, device_id=where, device_id_type=MESH)

    for j in range(HID // 128):
        cols = slice(128 * j, 128 * j + 128)
        v = gate[:, cols].astype(jnp.float32)
        u = up[:, cols].astype(jnp.float32)
        h = v / (1.0 + jnp.exp(-v)) * u
        hown[cols, :] = h.T.astype(jnp.bfloat16)

    pbuf[...] = jnp.zeros_like(pbuf)
    pl.semaphore_wait(barrier, len(partners))

    def grad_at(p, xs):
        if p == 0:
            rows, lo, n = pl.ds(pl.multiple_of(core * HR + y * TR, TR), TR), 0, CS
        else:
            rows, lo, n = pl.ds(pl.multiple_of(core * HR, HR), HR), CS, NB - CS
        return grad.at[rows, pl.ds(pl.multiple_of(xs * NB + lo, 128), n)]

    def part_at(p, zc, lo=0, n=NX):
        return quarter(zc, 0, lo, n) if p == 0 else rest(zc, lo, n)

    own_g = []
    for p in range(2):
        for k in (1, 3, 2):
            dst = part_at(p, z, x, 1)
            send(grad_at(p, xo(k)), dst.at[0], gx_s.at[p, k], gx_r.at[p, k], at_x(k))
        own_g.append(pltpu.make_async_copy(grad_at(p, x), part_at(p, z, x, 1).at[0], own_sem.at[p]))
        own_g[p].start()

    def hown_at(zc):
        return hown.at[pl.ds(pl.multiple_of(zc * MB, 16), MB), :]

    own_h = pltpu.make_async_copy(hown_at(z), hb.at[x, z], own_sem.at[2])
    own_h.start()

    def start_hz(k):
        send(hown_at(zo(k)), hb.at[x, z], hz_s.at[k], hz_r.at[k], at_z(k))

    def to_sib(part, slot, o):
        send(part, part, sib_s.at[slot, o], sib_r.at[slot, o], at_t(sib))

    def g_z(p, i):
        o = ORDER[i]
        zc = zo(o)

        def come(way, step, lo, n):
            arrived(part_at(p, zc, lo, n), gz_s.at[way, step, p], gz_r.at[way, step, p])

        def go(way, step, lo, n):
            part = part_at(p, zc, lo, n)
            send(part, part, gz_s.at[way, step, p], gz_r.at[way, step, p], at_z(1 if way == 0 else 7))

        if o == 0:
            own_g[p].wait()
            for k in range(1, NX):
                arrived(part_at(p, z, xo(NX - k), 1).at[0], gx_s.at[p, k], gx_r.at[p, k])
            go(0, 1, 0, NX)
            go(1, 1, 0, NX)
        elif o == 4:
            come(0, 4, 0, 2)
            come(1, 4, 2, 2)
        else:
            way, step = (0, 8 - o) if o > 4 else (1, o)
            come(way, step, 0, NX)
            if step < 3:
                go(way, step + 1, 0, NX)
            else:
                go(way, 4, 2 * way, 2)
        if p == 0:
            part = quarter(zc, 0)
            send(part, part, gy_s.at[0, o], gy_r.at[0, o], at_t(yo(1)))
            send(part, part, gy_s.at[1, o], gy_r.at[1, o], at_t(yo(3)))
        to_sib(part_at(p, zc), p, o)

    def g_y(i):
        o = ORDER[i]
        zc = zo(o)
        for way in range(2):
            source = 3 if way == 0 else 1
            arrived(quarter(zc, source), gy_s.at[way, o], gy_r.at[way, o])
            part = quarter(zc, source, 2 * way, 2)
            send(part, part, gy_s.at[2 + way, o], gy_r.at[2 + way, o], at_t(yo(4 - source)))
            to_sib(quarter(zc, source), 2 + way, o)

    def g_far(i):
        o = ORDER[i]
        zc = zo(o)
        for way in range(2):
            part = quarter(zc, 2, 2 * way, 2)
            arrived(part, gy_s.at[2 + way, o], gy_r.at[2 + way, o])
            to_sib(part, 4 + way, o)

    def h_z(i):
        o = ORDER[i]
        zc = zo(o)
        if o == 0:
            own_h.wait()
        else:
            arrived(hb.at[x, zc], hz_s.at[8 - o], hz_r.at[8 - o])
        send(hb.at[x, zc], hb.at[x, zc], hx_s.at[0, o], hx_r.at[0, o], at_x(1))
        send(hb.at[x, zc], hb.at[x, zc], hx_s.at[1, o], hx_r.at[1, o], at_x(3))

    def h_x(i):
        o = ORDER[i]
        zc = zo(o)
        for way in range(2):
            xs = xo(3 if way == 0 else 1)
            arrived(hb.at[xs, zc], hx_s.at[way, o], hx_r.at[way, o])
            half = hb.at[xs, zc, pl.ds(way * (MB // 2), MB // 2), :]
            send(half, half, hx_s.at[2 + way, o], hx_r.at[2 + way, o], at_x(1 if way == 0 else 3))

    def finish(i):
        o = ORDER[i]
        zc = zo(o)
        for way in range(2):
            half = hb.at[xo(2), zc, pl.ds(way * (MB // 2), MB // 2), :]
            arrived(half, hx_s.at[2 + way, o], hx_r.at[2 + way, o])
        c = 1 - core
        parts = [quarter(zc, 0, c=c), rest(zc, c=c), quarter(zc, 3, c=c), quarter(zc, 1, c=c)]
        parts += [quarter(zc, 2, 0, 2, c=c), quarter(zc, 2, 2, 2, c=c)]
        for slot, part in enumerate(parts):
            arrived(part, sib_s.at[slot, o], sib_r.at[slot, o])

        def product(k, _):
            xx = lax.div(k, 4)
            cols = pl.ds(pl.multiple_of(lax.rem(k, 4) * 256, 256), 256)
            leaf[zc, xx, :, cols] = jnp.dot(hb[xx, zc], gb[xx, zc, :, cols], preferred_element_type=jnp.float32)
            return 0

        lax.fori_loop(0, 16, product, 0)

        def products(za, zb, pairs):
            def gram(k, sums):
                rows = pl.ds(pl.multiple_of(k * 8, 8), 8)
                for c in range(NB // 128):
                    cols = slice(128 * c, 128 * c + 128)
                    a = [leaf[za, xx, rows, cols] for xx in range(NX)]
                    b = a if za is zb else [leaf[zb, xx, rows, cols] for xx in range(NX)]
                    sums = tuple(s + a[m] * b[n] for s, (m, n) in zip(sums, pairs))
                return sums

            return lax.fori_loop(0, MB // 8, gram, (jnp.zeros((8, 128), jnp.float32),) * len(pairs))

        def keep(m, n, low, gap, value):
            pbuf[pl.ds((m * 4 + n) * 64 + gap * 8 + low, 1), :] = jnp.sum(value, axis=0, keepdims=True)

        for (m, n), value in zip(PAIRS4, products(zc, zc, PAIRS4)):
            keep(m, n, zc, 0, value)
            if m != n:
                keep(n, m, zc, 0, value)
        for other in done:
            zd = zo(other)
            low, first = jnp.minimum(zc, zd), jnp.where(zc < zd, 1, 0)
            gap = zc + zd - 2 * low
            for (m, n), value in zip(ALL4, products(zc, zd, ALL4)):
                keep(first * m + (1 - first) * n, first * n + (1 - first) * m, low, gap, value)
        done.append(o)

    def all_sum(value):
        for phase, (count, me) in enumerate(((NT, t), (NX, x), (NZ, z))):
            slots = ar.at[phase]
            slots[me] = value
            for k in range(1, count):
                where = (at_t(to(k)), at_x(k), at_z(k))[phase]
                send(slots.at[me], slots.at[me], ar_s.at[phase, k], ar_r.at[phase, k], where)
            for k in range(1, count):
                arrived(slots.at[lax.rem(me + count - k, count)], ar_s.at[phase, k], ar_r.at[phase, k])
            value = jnp.sum(slots[0:count], axis=0)
        return value

    stages = {
        "s": start_hz, "q": functools.partial(g_z, 0), "r": functools.partial(g_z, 1), "y": g_y, "f": g_far,
        "h": h_z, "x": h_x, "c": finish,
    }
    for step in SCHEDULE:
        stages[step[0]](int(step[1]))

    tile = all_sum(
        jnp.concatenate(
            [jnp.sum(pbuf[128 * k:128 * k + 128, :].T, axis=0, keepdims=True) for k in range(8)], axis=0
        )
    )
    spread = [jnp.broadcast_to(tile[k:k + 1], (128, 128)).T for k in range(8)]
    table = [spread[k // 2][64 * (k % 2):64 * (k % 2) + 64] for k in range(16)]
    lower = tree_weights({(m, n): table[m * 4 + n][0:8] for m, n in PAIRS4}, 4)
    nodes = []
    for gap in range(NZ):
        shifted = [w if gap == 0 else jnp.concatenate([w[gap:], w[:gap]], axis=0) for w in lower]
        rows = slice(8 * gap, 8 * gap + 8)
        total = None
        for m in range(4):
            inner = sum(shifted[n] * table[m * 4 + n][rows] for n in range(4))
            total = lower[m] * inner if total is None else total + lower[m] * inner
        nodes.append(total)
    upper = tree_weights({(i, j): nodes[j - i][i:i + 1] for i, j in PAIRS8}, 8)
    for zz in range(NZ):
        for xx in range(NX):
            wbuf[zz * 4 + xx] = jnp.broadcast_to(lower[xx][zz:zz + 1] * upper[zz], (8, 128))

    for k in (4, 3, 5, 2, 6, 1, 7, 0):
        cols = pl.ds(pl.multiple_of(zo(k) * 128, 128), 128)

        def combine(g, _, k=k, cols=cols):
            totals = [jnp.zeros((8, 128), jnp.float32)] * 4
            for r in range(NZ * NX):
                w = wbuf[r]
                for q in range(4):
                    rows = pl.ds(pl.multiple_of(g * 32 + 8 * q, 8), 8)
                    totals[q] = totals[q] + w * leaf[r // 4, r % 4, rows, cols]
            block = jnp.concatenate(totals, axis=0).astype(jnp.bfloat16)
            cst[k, pl.ds(pl.multiple_of(g * 32, 32), 32), :] = block
            return 0

        lax.fori_loop(0, MB // 32, combine, 0)
        if k:
            send(cst.at[k], obuf.at[z], oz_s.at[k], oz_r.at[k], at_z(k))
    out[pl.ds(pl.multiple_of(z * MB, 16), MB), :] = cst[0]
    for k in range(1, NZ):
        zs = zo(NZ - k)
        arrived(obuf.at[zs], oz_s.at[k], oz_r.at[k])
        out[pl.ds(pl.multiple_of(zs * MB, 16), MB), :] = obuf[zs]
    for copy in sent:
        copy.wait_send()


def body(gate_input, up_input, grad_out):
    dma = pltpu.SemaphoreType.DMA
    vmem = pl.BlockSpec(memory_space=pltpu.VMEM)
    return pl.pallas_call(
        kernel,
        out_shape=jax.ShapeDtypeStruct((HID, 128), jnp.bfloat16),
        in_specs=[vmem, vmem, pl.BlockSpec(memory_space=pl.ANY)],
        out_specs=vmem,
        scratch_shapes=[
            pltpu.VMEM((HID, TOK), jnp.bfloat16),
            pltpu.VMEM((NX, NZ, MB, TOK), jnp.bfloat16),
            pltpu.VMEM((NX, NZ, TOK, NB), jnp.bfloat16),
            pltpu.VMEM((NZ, NX, MB, NB), jnp.float32),
            pltpu.VMEM((1024, 128), jnp.float32),
            pltpu.VMEM((NZ * NX, 8, 128), jnp.float32),
            pltpu.VMEM((3, 8, 8, 128), jnp.float32),
            pltpu.VMEM((NZ, MB, 128), jnp.bfloat16),
            pltpu.VMEM((NZ, MB, 128), jnp.bfloat16),
            dma((3,)),
            dma((2, NX)), dma((2, NX)),
            dma((NZ,)), dma((NZ,)),
            dma((2, 5, 2)), dma((2, 5, 2)),
            dma((4, NZ)), dma((4, NZ)),
            dma((6, NZ)), dma((6, NZ)),
            dma((4, NZ)), dma((4, NZ)),
            dma((3, 8)), dma((3, 8)),
            dma((NZ,)), dma((NZ,)),
        ],
        compiler_params=pltpu.CompilerParams(
            collective_id=0, has_side_effects=True, vmem_limit_bytes=62 * 1024 * 1024
        ),
        cost_estimate=pl.CostEstimate(flops=3_760_000_000, bytes_accessed=5_000_000, transcendentals=460_000),
    )(gate_input, up_input, grad_out)


def solution(mesh):
    placed = (P("dp", "tensor"), P("dp", "tensor"), P("dp", None))
    return jax.shard_map(
        body, mesh=mesh, in_specs=placed, out_specs=P("tensor", "dp"), check_vma=False
    )
```

```python
import functools

import jax
import jax.numpy as jnp
from jax import lax
from jax.experimental import pallas as pl
from jax.experimental.pallas import tpu as pltpu
from jax.sharding import PartitionSpec as P

epsilon = 1e-06
MESH = pl.DeviceIdType.MESH
NX, NZ, NT = 4, 8, 8
TOK = 256
HID = 1792
MB = HID // NZ
NB = 1024
TR = TOK // NT
HR = TOK // 2
DB = 1024
GB = 4
CS = 768
ORDER = (0, 7, 1, 6, 2, 5, 3, 4)
SCHEDULE = (
    "h0", "s1", "s7", "s2", "s6", "q0", "r0", "h1", "h2", "x0", "y0", "h3", "h4", "x1", "x2", "f0",
    "q1", "q2", "x3", "x4", "c0", "y1", "r1", "r2", "y2", "f1",
    "q3", "q4", "s3", "s5", "f2", "c1", "y3", "r3", "r4", "c2", "y4", "f3",
    "q5", "q6", "s4", "f4", "h5", "h6", "c3", "x5", "y5", "r5", "r6", "x6", "y6", "c4",
    "q7", "f5", "r7", "f6", "h7", "c5", "y7", "x7", "c6", "f7", "c7",
)
TREE_BITS = (2, 1, 16, 8, 4)


def pair_coef(aa, bb, ab):
    aa, bb = jnp.maximum(aa, 0.0), jnp.maximum(bb, 0.0)
    bound = jnp.sqrt(aa) * jnp.sqrt(bb)
    return 1.0 - jnp.clip(ab, -bound, bound) / (2.0 * (aa + epsilon))


def swap(value, index, bit, axis):
    size = value.shape[axis]
    return jnp.where(
        (index & bit) != 0, pltpu.roll(value, bit, axis), pltpu.roll(value, size - bit, axis)
    )


def leaf_weights(gram):
    row = lax.broadcasted_iota(jnp.int32, gram.shape, 0)
    lane = lax.broadcasted_iota(jnp.int32, gram.shape, 1)
    weights = jnp.ones(gram.shape, jnp.float32)
    for bit in TREE_BITS:
        own = jnp.where(row == lane, gram, 0.0)
        pair = jnp.where((row ^ bit) == lane, gram, 0.0)
        far = swap(own, row, bit, 0)
        far_t = swap(own, lane, bit, 1)
        down = pair_coef(
            jnp.sum(own, axis=1, keepdims=True), jnp.sum(far, axis=1, keepdims=True),
            jnp.sum(pair, axis=1, keepdims=True),
        )
        across = pair_coef(
            jnp.sum(own, axis=0, keepdims=True), jnp.sum(far_t, axis=0, keepdims=True),
            jnp.sum(pair, axis=0, keepdims=True),
        )
        weights = weights * down
        gram = gram * down * across
        gram = gram + swap(gram, row, bit, 0)
        gram = gram + swap(gram, lane, bit, 1)
    return weights


def kernel(
    gate, up, grad, out,
    hown, hb, gb, leaf, acc, wbuf, ar, cst, obuf,
    own_sem, gx_s, gx_r, hz_s, hz_r, gz_s, gz_r, gy_s, gy_r, sib_s, sib_r, hx_s, hx_r, ar_s, ar_r, oz_s, oz_r,
):
    dp = lax.axis_index("dp")
    t = lax.axis_index("tensor")
    x, z = lax.div(dp, NZ), lax.rem(dp, NZ)
    y, core = lax.div(t, 2), lax.rem(t, 2)
    sib = y * 2 + 1 - core

    def xo(k):
        return lax.rem(x + k, NX)

    def zo(k):
        return lax.rem(z + k, NZ)

    def to(k):
        return lax.rem(t + k, NT)

    def yo(k):
        return lax.rem(y + k, 4) * 2 + core

    def at_x(k):
        return (xo(k) * NZ + z, t)

    def at_z(k):
        return (x * NZ + zo(k), t)

    def at_t(rank):
        return (dp, rank)

    def remote(src, dst, send, recv, where):
        return pltpu.make_async_remote_copy(
            src_ref=src, dst_ref=dst, send_sem=send, recv_sem=recv, device_id=where, device_id_type=MESH
        )

    sent = []

    def send(src, dst, ss, rs, where):
        copy = remote(src, dst, ss, rs, where)
        copy.start()
        sent.append(copy)

    def arrived(dst, ss, rs):
        remote(dst, dst, ss, rs, at_x(1)).wait_recv()

    def quarter(zc, yy, lo=0, n=NX, c=core):
        rows = pl.ds(pl.multiple_of(c * HR + lax.rem(y + yy, 4) * TR, TR), TR)
        return gb.at[pl.ds(lo, n), zc, rows, pl.ds(0, CS)]

    def rest(zc, lo=0, n=NX, c=core):
        return gb.at[pl.ds(lo, n), zc, pl.ds(pl.multiple_of(c * HR, HR), HR), pl.ds(CS, NB - CS)]

    barrier = pltpu.get_barrier_semaphore()
    partners = [at_x(k) for k in range(1, NX)] + [at_z(k) for k in range(1, NZ)] + [at_t(to(k)) for k in range(1, NT)]
    for where in partners:
        pl.semaphore_signal(barrier, inc=1, device_id=where, device_id_type=MESH)

    for j in range(HID // 128):
        cols = slice(128 * j, 128 * j + 128)
        v = gate[:, cols].astype(jnp.float32)
        u = up[:, cols].astype(jnp.float32)
        h = v / (1.0 + jnp.exp(-v)) * u
        hown[cols, :] = h.T.astype(jnp.bfloat16)

    pl.semaphore_wait(barrier, len(partners))

    def grad_at(p, xs):
        if p == 0:
            rows, lo, n = pl.ds(pl.multiple_of(core * HR + y * TR, TR), TR), 0, CS
        else:
            rows, lo, n = pl.ds(pl.multiple_of(core * HR, HR), HR), CS, NB - CS
        return grad.at[rows, pl.ds(pl.multiple_of(xs * NB + lo, 128), n)]

    def part_at(p, zc, lo=0, n=NX):
        return quarter(zc, 0, lo, n) if p == 0 else rest(zc, lo, n)

    own_g = []
    for p in range(2):
        for k in (1, 3, 2):
            dst = part_at(p, z, x, 1)
            send(grad_at(p, xo(k)), dst.at[0], gx_s.at[p, k], gx_r.at[p, k], at_x(k))
        own_g.append(pltpu.make_async_copy(grad_at(p, x), part_at(p, z, x, 1).at[0], own_sem.at[p]))
        own_g[p].start()

    def hown_at(zc):
        return hown.at[pl.ds(pl.multiple_of(zc * MB, 16), MB), :]

    own_h = pltpu.make_async_copy(hown_at(z), hb.at[x, z], own_sem.at[2])
    own_h.start()

    def start_hz(k):
        send(hown_at(zo(k)), hb.at[x, z], hz_s.at[k], hz_r.at[k], at_z(k))

    def to_sib(part, slot, o):
        send(part, part, sib_s.at[slot, o], sib_r.at[slot, o], at_t(sib))

    def g_z(p, i):
        o = ORDER[i]
        zc = zo(o)

        def come(way, step, lo, n):
            arrived(part_at(p, zc, lo, n), gz_s.at[way, step, p], gz_r.at[way, step, p])

        def go(way, step, lo, n):
            part = part_at(p, zc, lo, n)
            send(part, part, gz_s.at[way, step, p], gz_r.at[way, step, p], at_z(1 if way == 0 else 7))

        if o == 0:
            own_g[p].wait()
            for k in range(1, NX):
                arrived(part_at(p, z, xo(NX - k), 1).at[0], gx_s.at[p, k], gx_r.at[p, k])
            go(0, 1, 0, NX)
            go(1, 1, 0, NX)
        elif o == 4:
            come(0, 4, 0, 2)
            come(1, 4, 2, 2)
        else:
            way, step = (0, 8 - o) if o > 4 else (1, o)
            come(way, step, 0, NX)
            if step < 3:
                go(way, step + 1, 0, NX)
            else:
                go(way, 4, 2 * way, 2)
        if p == 0:
            part = quarter(zc, 0)
            send(part, part, gy_s.at[0, o], gy_r.at[0, o], at_t(yo(1)))
            send(part, part, gy_s.at[1, o], gy_r.at[1, o], at_t(yo(3)))
        to_sib(part_at(p, zc), p, o)

    def g_y(i):
        o = ORDER[i]
        zc = zo(o)
        for way in range(2):
            source = 3 if way == 0 else 1
            arrived(quarter(zc, source), gy_s.at[way, o], gy_r.at[way, o])
            part = quarter(zc, source, 2 * way, 2)
            send(part, part, gy_s.at[2 + way, o], gy_r.at[2 + way, o], at_t(yo(4 - source)))
            to_sib(quarter(zc, source), 2 + way, o)

    def g_far(i):
        o = ORDER[i]
        zc = zo(o)
        for way in range(2):
            part = quarter(zc, 2, 2 * way, 2)
            arrived(part, gy_s.at[2 + way, o], gy_r.at[2 + way, o])
            to_sib(part, 4 + way, o)

    def h_z(i):
        o = ORDER[i]
        zc = zo(o)
        if o == 0:
            own_h.wait()
        else:
            arrived(hb.at[x, zc], hz_s.at[8 - o], hz_r.at[8 - o])
        send(hb.at[x, zc], hb.at[x, zc], hx_s.at[0, o], hx_r.at[0, o], at_x(1))
        send(hb.at[x, zc], hb.at[x, zc], hx_s.at[1, o], hx_r.at[1, o], at_x(3))

    def h_x(i):
        o = ORDER[i]
        zc = zo(o)
        for way in range(2):
            xs = xo(3 if way == 0 else 1)
            arrived(hb.at[xs, zc], hx_s.at[way, o], hx_r.at[way, o])
            half = hb.at[xs, zc, pl.ds(way * (MB // 2), MB // 2), :]
            send(half, half, hx_s.at[2 + way, o], hx_r.at[2 + way, o], at_x(1 if way == 0 else 3))

    def finish(i):
        o = ORDER[i]
        zc = zo(o)
        for way in range(2):
            half = hb.at[xo(2), zc, pl.ds(way * (MB // 2), MB // 2), :]
            arrived(half, hx_s.at[2 + way, o], hx_r.at[2 + way, o])
        c = 1 - core
        parts = [quarter(zc, 0, c=c), rest(zc, c=c), quarter(zc, 3, c=c), quarter(zc, 1, c=c)]
        parts += [quarter(zc, 2, 0, 2, c=c), quarter(zc, 2, 2, 2, c=c)]
        for slot, part in enumerate(parts):
            arrived(part, sib_s.at[slot, o], sib_r.at[slot, o])

        def product(k, _):
            xx = 2 * lax.div(k, NB // DB)
            cols = pl.ds(pl.multiple_of(lax.rem(k, NB // DB) * DB, DB), DB)
            first, second = (
                jnp.dot(hb[xx + m, zc], gb[xx + m, zc, :, cols], preferred_element_type=jnp.float32) for m in range(2)
            )
            rows = pl.ds(pl.multiple_of(zc * 32 + xx * 8, 16), 16)
            for g in range(MB // 8):
                both = jnp.concatenate([first[8 * g:8 * g + 8], second[8 * g:8 * g + 8]], axis=0)
                leaf[g, rows, cols] = both.astype(jnp.bfloat16)
            return 0

        lax.fori_loop(0, 2 * NB // DB, product, 0)

    def all_sum(value):
        for phase, (count, me) in enumerate(((NT, t), (NX, x), (NZ, z))):
            slots = ar.at[phase]
            slots[me] = value
            for k in range(1, count):
                where = (at_t(to(k)), at_x(k), at_z(k))[phase]
                send(slots.at[me], slots.at[me], ar_s.at[phase, k], ar_r.at[phase, k], where)
            for k in range(1, count):
                arrived(slots.at[lax.rem(me + count - k, count)], ar_s.at[phase, k], ar_r.at[phase, k])
            value = jnp.sum(slots[0:count], axis=0)
        return value

    stages = {
        "s": start_hz, "q": functools.partial(g_z, 0), "r": functools.partial(g_z, 1), "y": g_y, "f": g_far,
        "h": h_z, "x": h_x, "c": finish,
    }
    for step in SCHEDULE:
        stages[step[0]](int(step[1]))

    acc[...] = jnp.zeros_like(acc)

    def gram(k, _):
        total = None
        for g in range(GB):
            rows = leaf[k * GB + g]
            part = lax.dot_general(rows, rows, (((1,), (1,)), ((), ())), preferred_element_type=jnp.float32)
            total = part if total is None else total + part
        acc[...] += total
        return 0

    lax.fori_loop(0, MB // 8 // GB, gram, 0)
    index = [lax.broadcasted_iota(jnp.int32, (256, 256), axis) for axis in range(2)]
    like = jnp.where(lax.rem(index[0], 8) == lax.rem(index[1], 8), acc[...], 0.0)
    like = jnp.sum(like.reshape(32, 8, 256), axis=1)
    index = [lax.broadcasted_iota(jnp.int32, (256, 128), axis) for axis in range(2)]
    pick = jnp.where(lax.div(index[0], 8) == index[1], 1.0, 0.0).astype(jnp.float32)
    local = jnp.dot(like, pick, precision=lax.Precision.HIGHEST, preferred_element_type=jnp.float32)
    tile = local[0:8]
    for q in range(1, 4):
        tile = tile + pltpu.roll(local[8 * q:8 * q + 8], 32 * q, 1)
    tile = all_sum(tile)
    lane = lax.broadcasted_iota(jnp.int32, (8, 128), 1)
    total = [tile] + [pltpu.roll(tile, 128 - 32 * q, 1) for q in range(1, 4)]
    weights = leaf_weights(jnp.concatenate([jnp.where(lane < 32, part, 0.0) for part in total], axis=0))
    for r in range(NZ * NX):
        wbuf[r] = jnp.broadcast_to(weights[r:r + 1], (8, 128))

    for k in (4, 3, 5, 2, 6, 1, 7, 0):
        cols = pl.ds(pl.multiple_of(zo(k) * 128, 128), 128)

        def combine(g, _, k=k, cols=cols):
            totals = [jnp.zeros((8, 128), jnp.float32)] * 4
            for r in range(0, NZ * NX, 2):
                for q in range(4):
                    both = leaf[g * 4 + q, 8 * r:8 * r + 16, cols].astype(jnp.float32)
                    totals[q] = totals[q] + wbuf[r] * both[0:8] + wbuf[r + 1] * both[8:16]
            block = jnp.concatenate(totals, axis=0).astype(jnp.bfloat16)
            cst[k, pl.ds(pl.multiple_of(g * 32, 32), 32), :] = block
            return 0

        lax.fori_loop(0, MB // 32, combine, 0)
        if k:
            send(cst.at[k], obuf.at[z], oz_s.at[k], oz_r.at[k], at_z(k))
    out[pl.ds(pl.multiple_of(z * MB, 16), MB), :] = cst[0]
    for k in range(1, NZ):
        zs = zo(NZ - k)
        arrived(obuf.at[zs], oz_s.at[k], oz_r.at[k])
        out[pl.ds(pl.multiple_of(zs * MB, 16), MB), :] = obuf[zs]
    for copy in sent:
        copy.wait_send()


def body(gate_input, up_input, grad_out):
    dma = pltpu.SemaphoreType.DMA
    vmem = pl.BlockSpec(memory_space=pltpu.VMEM)
    return pl.pallas_call(
        kernel,
        out_shape=jax.ShapeDtypeStruct((HID, 128), jnp.bfloat16),
        in_specs=[vmem, vmem, pl.BlockSpec(memory_space=pl.ANY)],
        out_specs=vmem,
        scratch_shapes=[
            pltpu.VMEM((HID, TOK), jnp.bfloat16),
            pltpu.VMEM((NX, NZ, MB, TOK), jnp.bfloat16),
            pltpu.VMEM((NX, NZ, TOK, NB), jnp.bfloat16),
            pltpu.VMEM((MB // 8, 256, NB), jnp.bfloat16),
            pltpu.VMEM((256, 256), jnp.float32),
            pltpu.VMEM((NZ * NX, 8, 128), jnp.float32),
            pltpu.VMEM((3, 8, 8, 128), jnp.float32),
            pltpu.VMEM((NZ, MB, 128), jnp.bfloat16),
            pltpu.VMEM((NZ, MB, 128), jnp.bfloat16),
            dma((3,)),
            dma((2, NX)), dma((2, NX)),
            dma((NZ,)), dma((NZ,)),
            dma((2, 5, 2)), dma((2, 5, 2)),
            dma((4, NZ)), dma((4, NZ)),
            dma((6, NZ)), dma((6, NZ)),
            dma((4, NZ)), dma((4, NZ)),
            dma((3, 8)), dma((3, 8)),
            dma((NZ,)), dma((NZ,)),
        ],
        compiler_params=pltpu.CompilerParams(
            collective_id=0, has_side_effects=True, vmem_limit_bytes=62 * 1024 * 1024
        ),
        cost_estimate=pl.CostEstimate(flops=3_760_000_000, bytes_accessed=5_000_000, transcendentals=460_000),
    )(gate_input, up_input, grad_out)


def solution(mesh):
    placed = (P("dp", "tensor"), P("dp", "tensor"), P("dp", None))
    return jax.shard_map(
        body, mesh=mesh, in_specs=placed, out_specs=P("tensor", "dp"), check_vma=False
    )
```

```python
import functools

import jax
import jax.numpy as jnp
from jax import lax
from jax.experimental import pallas as pl
from jax.experimental.pallas import tpu as pltpu
from jax.sharding import PartitionSpec as P

epsilon = 1e-06
MESH = pl.DeviceIdType.MESH
NX, NZ, NT = 4, 8, 8
TOK = 256
HID = 1792
MB = HID // NZ
NB = 1024
TR = TOK // NT
HR = TOK // 2
DB = 1024
GB = 14
CS = 768
ORDER = (0, 7, 1, 6, 2, 5, 3, 4)
SCHEDULE = (
    "h0", "s1", "s7", "s2", "s6", "q0", "r0", "h1", "h2", "x0", "y0", "h3", "h4", "x1", "x2", "f0",
    "q1", "q2", "x3", "x4", "c0", "y1", "r1", "r2", "y2", "f1",
    "q3", "q4", "s3", "s5", "f2", "c1", "y3", "r3", "r4", "c2", "y4", "f3",
    "q5", "q6", "s4", "f4", "h5", "h6", "c3", "x5", "y5", "r5", "r6", "x6", "y6", "c4",
    "q7", "f5", "r7", "f6", "h7", "c5", "y7", "x7", "c6", "f7", "c7",
)
TREE_BITS = (2, 1, 16, 8, 4)


def pair_coef(aa, bb, ab):
    aa, bb = jnp.maximum(aa, 0.0), jnp.maximum(bb, 0.0)
    bound = jnp.sqrt(aa) * jnp.sqrt(bb)
    return 1.0 - jnp.clip(ab, -bound, bound) / (2.0 * (aa + epsilon))


def swap(value, index, bit, axis):
    size = value.shape[axis]
    return jnp.where(
        (index & bit) != 0, pltpu.roll(value, bit, axis), pltpu.roll(value, size - bit, axis)
    )


def leaf_weights(gram):
    row = lax.broadcasted_iota(jnp.int32, gram.shape, 0)
    lane = lax.broadcasted_iota(jnp.int32, gram.shape, 1)
    weights = jnp.ones(gram.shape, jnp.float32)
    for bit in TREE_BITS:
        own = jnp.where(row == lane, gram, 0.0)
        pair = jnp.where((row ^ bit) == lane, gram, 0.0)
        far = swap(own, row, bit, 0)
        far_t = swap(own, lane, bit, 1)
        down = pair_coef(
            jnp.sum(own, axis=1, keepdims=True), jnp.sum(far, axis=1, keepdims=True),
            jnp.sum(pair, axis=1, keepdims=True),
        )
        across = pair_coef(
            jnp.sum(own, axis=0, keepdims=True), jnp.sum(far_t, axis=0, keepdims=True),
            jnp.sum(pair, axis=0, keepdims=True),
        )
        weights = weights * down
        gram = gram * down * across
        gram = gram + swap(gram, row, bit, 0)
        gram = gram + swap(gram, lane, bit, 1)
    return weights


def kernel(
    gate, up, grad, out,
    hown, hb, gb, leaf, acc, wbuf, ar, cst, obuf,
    own_sem, gx_s, gx_r, hz_s, hz_r, gz_s, gz_r, gy_s, gy_r, sib_s, sib_r, hx_s, hx_r, ar_s, ar_r, oz_s, oz_r,
):
    dp = lax.axis_index("dp")
    t = lax.axis_index("tensor")
    x, z = lax.div(dp, NZ), lax.rem(dp, NZ)
    y, core = lax.div(t, 2), lax.rem(t, 2)
    sib = y * 2 + 1 - core

    def xo(k):
        return lax.rem(x + k, NX)

    def zo(k):
        return lax.rem(z + k, NZ)

    def to(k):
        return lax.rem(t + k, NT)

    def yo(k):
        return lax.rem(y + k, 4) * 2 + core

    def at_x(k):
        return (xo(k) * NZ + z, t)

    def at_z(k):
        return (x * NZ + zo(k), t)

    def at_t(rank):
        return (dp, rank)

    def remote(src, dst, send, recv, where):
        return pltpu.make_async_remote_copy(
            src_ref=src, dst_ref=dst, send_sem=send, recv_sem=recv, device_id=where, device_id_type=MESH
        )

    sent = []

    def send(src, dst, ss, rs, where):
        copy = remote(src, dst, ss, rs, where)
        copy.start()
        sent.append(copy)

    def arrived(dst, ss, rs):
        remote(dst, dst, ss, rs, at_x(1)).wait_recv()

    def quarter(zc, yy, lo=0, n=NX, c=core):
        rows = pl.ds(pl.multiple_of(c * HR + lax.rem(y + yy, 4) * TR, TR), TR)
        return gb.at[pl.ds(lo, n), zc, rows, pl.ds(0, CS)]

    def rest(zc, lo=0, n=NX, c=core):
        return gb.at[pl.ds(lo, n), zc, pl.ds(pl.multiple_of(c * HR, HR), HR), pl.ds(CS, NB - CS)]

    barrier = pltpu.get_barrier_semaphore()
    partners = [at_x(k) for k in range(1, NX)] + [at_z(k) for k in range(1, NZ)] + [at_t(to(k)) for k in range(1, NT)]
    for where in partners:
        pl.semaphore_signal(barrier, inc=1, device_id=where, device_id_type=MESH)

    for j in range(HID // 128):
        cols = slice(128 * j, 128 * j + 128)
        v = gate[:, cols].astype(jnp.float32)
        u = up[:, cols].astype(jnp.float32)
        h = v / (1.0 + jnp.exp(-v)) * u
        hown[cols, :] = h.T.astype(jnp.bfloat16)

    pl.semaphore_wait(barrier, len(partners))

    def grad_at(p, xs):
        if p == 0:
            rows, lo, n = pl.ds(pl.multiple_of(core * HR + y * TR, TR), TR), 0, CS
        else:
            rows, lo, n = pl.ds(pl.multiple_of(core * HR, HR), HR), CS, NB - CS
        return grad.at[rows, pl.ds(pl.multiple_of(xs * NB + lo, 128), n)]

    def part_at(p, zc, lo=0, n=NX):
        return quarter(zc, 0, lo, n) if p == 0 else rest(zc, lo, n)

    own_g = []
    for p in range(2):
        for k in (1, 3, 2):
            dst = part_at(p, z, x, 1)
            send(grad_at(p, xo(k)), dst.at[0], gx_s.at[p, k], gx_r.at[p, k], at_x(k))
        own_g.append(pltpu.make_async_copy(grad_at(p, x), part_at(p, z, x, 1).at[0], own_sem.at[p]))
        own_g[p].start()

    def hown_at(zc):
        return hown.at[pl.ds(pl.multiple_of(zc * MB, 16), MB), :]

    own_h = pltpu.make_async_copy(hown_at(z), hb.at[x, z], own_sem.at[2])
    own_h.start()

    def start_hz(k):
        send(hown_at(zo(k)), hb.at[x, z], hz_s.at[k], hz_r.at[k], at_z(k))

    def to_sib(part, slot, o):
        send(part, part, sib_s.at[slot, o], sib_r.at[slot, o], at_t(sib))

    def g_z(p, i):
        o = ORDER[i]
        zc = zo(o)

        def come(way, step, lo, n):
            arrived(part_at(p, zc, lo, n), gz_s.at[way, step, p], gz_r.at[way, step, p])

        def go(way, step, lo, n):
            part = part_at(p, zc, lo, n)
            send(part, part, gz_s.at[way, step, p], gz_r.at[way, step, p], at_z(1 if way == 0 else 7))

        if o == 0:
            own_g[p].wait()
            for k in range(1, NX):
                arrived(part_at(p, z, xo(NX - k), 1).at[0], gx_s.at[p, k], gx_r.at[p, k])
            go(0, 1, 0, NX)
            go(1, 1, 0, NX)
        elif o == 4:
            come(0, 4, 0, 2)
            come(1, 4, 2, 2)
        else:
            way, step = (0, 8 - o) if o > 4 else (1, o)
            come(way, step, 0, NX)
            if step < 3:
                go(way, step + 1, 0, NX)
            else:
                go(way, 4, 2 * way, 2)
        if p == 0:
            part = quarter(zc, 0)
            send(part, part, gy_s.at[0, o], gy_r.at[0, o], at_t(yo(1)))
            send(part, part, gy_s.at[1, o], gy_r.at[1, o], at_t(yo(3)))
        to_sib(part_at(p, zc), p, o)

    def g_y(i):
        o = ORDER[i]
        zc = zo(o)
        for way in range(2):
            source = 3 if way == 0 else 1
            arrived(quarter(zc, source), gy_s.at[way, o], gy_r.at[way, o])
            part = quarter(zc, source, 2 * way, 2)
            send(part, part, gy_s.at[2 + way, o], gy_r.at[2 + way, o], at_t(yo(4 - source)))
            to_sib(quarter(zc, source), 2 + way, o)

    def g_far(i):
        o = ORDER[i]
        zc = zo(o)
        for way in range(2):
            part = quarter(zc, 2, 2 * way, 2)
            arrived(part, gy_s.at[2 + way, o], gy_r.at[2 + way, o])
            to_sib(part, 4 + way, o)

    def h_z(i):
        o = ORDER[i]
        zc = zo(o)
        if o == 0:
            own_h.wait()
        else:
            arrived(hb.at[x, zc], hz_s.at[8 - o], hz_r.at[8 - o])
        send(hb.at[x, zc], hb.at[x, zc], hx_s.at[0, o], hx_r.at[0, o], at_x(1))
        send(hb.at[x, zc], hb.at[x, zc], hx_s.at[1, o], hx_r.at[1, o], at_x(3))

    def h_x(i):
        o = ORDER[i]
        zc = zo(o)
        for way in range(2):
            xs = xo(3 if way == 0 else 1)
            arrived(hb.at[xs, zc], hx_s.at[way, o], hx_r.at[way, o])
            half = hb.at[xs, zc, pl.ds(way * (MB // 2), MB // 2), :]
            send(half, half, hx_s.at[2 + way, o], hx_r.at[2 + way, o], at_x(1 if way == 0 else 3))

    def finish(i):
        o = ORDER[i]
        zc = zo(o)
        for way in range(2):
            half = hb.at[xo(2), zc, pl.ds(way * (MB // 2), MB // 2), :]
            arrived(half, hx_s.at[2 + way, o], hx_r.at[2 + way, o])
        c = 1 - core
        parts = [quarter(zc, 0, c=c), rest(zc, c=c), quarter(zc, 3, c=c), quarter(zc, 1, c=c)]
        parts += [quarter(zc, 2, 0, 2, c=c), quarter(zc, 2, 2, 2, c=c)]
        for slot, part in enumerate(parts):
            arrived(part, sib_s.at[slot, o], sib_r.at[slot, o])

        def product(k, _):
            xx = 2 * lax.div(k, NB // DB)
            cols = pl.ds(pl.multiple_of(lax.rem(k, NB // DB) * DB, DB), DB)
            first, second = (
                jnp.dot(hb[xx + m, zc], gb[xx + m, zc, :, cols], preferred_element_type=jnp.float32) for m in range(2)
            )
            rows = pl.ds(pl.multiple_of(zc * 32 + xx * 8, 16), 16)
            for g in range(MB // 8):
                both = jnp.concatenate([first[8 * g:8 * g + 8], second[8 * g:8 * g + 8]], axis=0)
                leaf[g, rows, cols] = both.astype(jnp.bfloat16)
            return 0

        lax.fori_loop(0, 2 * NB // DB, product, 0)

    def all_sum(value):
        for phase, (count, me) in enumerate(((NT, t), (NX, x), (NZ, z))):
            slots = ar.at[phase]
            slots[me] = value
            for k in range(1, count):
                where = (at_t(to(k)), at_x(k), at_z(k))[phase]
                send(slots.at[me], slots.at[me], ar_s.at[phase, k], ar_r.at[phase, k], where)
            for k in range(1, count):
                arrived(slots.at[lax.rem(me + count - k, count)], ar_s.at[phase, k], ar_r.at[phase, k])
            value = jnp.sum(slots[0:count], axis=0)
        return value

    stages = {
        "s": start_hz, "q": functools.partial(g_z, 0), "r": functools.partial(g_z, 1), "y": g_y, "f": g_far,
        "h": h_z, "x": h_x, "c": finish,
    }
    for step in SCHEDULE:
        stages[step[0]](int(step[1]))

    acc[...] = jnp.zeros_like(acc)

    def gram(k, _):
        total = None
        for g in range(GB):
            rows = leaf[k * GB + g]
            part = lax.dot_general(rows, rows, (((1,), (1,)), ((), ())), preferred_element_type=jnp.float32)
            total = part if total is None else total + part
        acc[...] += total
        return 0

    lax.fori_loop(0, MB // 8 // GB, gram, 0)
    index = [lax.broadcasted_iota(jnp.int32, (256, 256), axis) for axis in range(2)]
    like = jnp.where(lax.rem(index[0], 8) == lax.rem(index[1], 8), acc[...], 0.0)
    like = jnp.sum(like.reshape(32, 8, 256), axis=1)
    index = [lax.broadcasted_iota(jnp.int32, (256, 128), axis) for axis in range(2)]
    pick = jnp.where(lax.div(index[0], 8) == index[1], 1.0, 0.0).astype(jnp.float32)
    local = jnp.dot(like, pick, precision=lax.Precision.HIGHEST, preferred_element_type=jnp.float32)
    tile = local[0:8]
    for q in range(1, 4):
        tile = tile + pltpu.roll(local[8 * q:8 * q + 8], 32 * q, 1)
    tile = all_sum(tile)
    lane = lax.broadcasted_iota(jnp.int32, (8, 128), 1)
    total = [tile] + [pltpu.roll(tile, 128 - 32 * q, 1) for q in range(1, 4)]
    weights = leaf_weights(jnp.concatenate([jnp.where(lane < 32, part, 0.0) for part in total], axis=0))
    for r in range(NZ * NX):
        wbuf[r] = jnp.broadcast_to(weights[r:r + 1], (8, 128))

    for k in (4, 3, 5, 2, 6, 1, 7, 0):
        cols = pl.ds(pl.multiple_of(zo(k) * 128, 128), 128)

        def combine(g, _, k=k, cols=cols):
            totals = [jnp.zeros((8, 128), jnp.float32)] * 4
            for r in range(0, NZ * NX, 2):
                for q in range(4):
                    both = leaf[g * 4 + q, 8 * r:8 * r + 16, cols].astype(jnp.float32)
                    totals[q] = totals[q] + wbuf[r] * both[0:8] + wbuf[r + 1] * both[8:16]
            block = jnp.concatenate(totals, axis=0).astype(jnp.bfloat16)
            cst[k, pl.ds(pl.multiple_of(g * 32, 32), 32), :] = block
            return 0

        lax.fori_loop(0, MB // 32, combine, 0)
        if k:
            send(cst.at[k], obuf.at[z], oz_s.at[k], oz_r.at[k], at_z(k))
    out[pl.ds(pl.multiple_of(z * MB, 16), MB), :] = cst[0]
    for k in range(1, NZ):
        zs = zo(NZ - k)
        arrived(obuf.at[zs], oz_s.at[k], oz_r.at[k])
        out[pl.ds(pl.multiple_of(zs * MB, 16), MB), :] = obuf[zs]
    for copy in sent:
        copy.wait_send()


def body(gate_input, up_input, grad_out):
    dma = pltpu.SemaphoreType.DMA
    vmem = pl.BlockSpec(memory_space=pltpu.VMEM)
    return pl.pallas_call(
        kernel,
        out_shape=pltpu.VMEM((HID, 128), jnp.bfloat16),
        in_specs=[vmem, vmem, pl.BlockSpec(memory_space=pl.ANY)],
        out_specs=vmem,
        scratch_shapes=[
            pltpu.VMEM((HID, TOK), jnp.bfloat16),
            pltpu.VMEM((NX, NZ, MB, TOK), jnp.bfloat16),
            pltpu.VMEM((NX, NZ, TOK, NB), jnp.bfloat16),
            pltpu.VMEM((MB // 8, 256, NB), jnp.bfloat16),
            pltpu.VMEM((256, 256), jnp.float32),
            pltpu.VMEM((NZ * NX, 8, 128), jnp.float32),
            pltpu.VMEM((3, 8, 8, 128), jnp.float32),
            pltpu.VMEM((NZ, MB, 128), jnp.bfloat16),
            pltpu.VMEM((NZ, MB, 128), jnp.bfloat16),
            dma((3,)),
            dma((2, NX)), dma((2, NX)),
            dma((NZ,)), dma((NZ,)),
            dma((2, 5, 2)), dma((2, 5, 2)),
            dma((4, NZ)), dma((4, NZ)),
            dma((6, NZ)), dma((6, NZ)),
            dma((4, NZ)), dma((4, NZ)),
            dma((3, 8)), dma((3, 8)),
            dma((NZ,)), dma((NZ,)),
        ],
        compiler_params=pltpu.CompilerParams(
            collective_id=0, has_side_effects=True, vmem_limit_bytes=62 * 1024 * 1024
        ),
        cost_estimate=pl.CostEstimate(flops=3_760_000_000, bytes_accessed=5_000_000, transcendentals=460_000),
    )(gate_input, up_input, grad_out)


def solution(mesh):
    placed = (P("dp", "tensor"), P("dp", "tensor"), P("dp", None))
    return jax.shard_map(
        body, mesh=mesh, in_specs=placed, out_specs=P("tensor", "dp"), check_vma=False
    )
```

```python
import functools

import jax
import jax.numpy as jnp
from jax import lax
from jax.experimental import pallas as pl
from jax.experimental.pallas import tpu as pltpu
from jax.sharding import PartitionSpec as P

epsilon = 1e-06
MESH = pl.DeviceIdType.MESH
NX, NZ, NT = 4, 8, 8
TOK = 256
HID = 1792
MB = HID // NZ
NB = 1024
TR = TOK // NT
HR = TOK // 2
GB = 14
CS = 768
ORDER = (0, 7, 1, 6, 2, 5, 3, 4)
SCHEDULE = (
    "h0", "s1", "s7", "s2", "s6", "q0", "r0", "h1", "h2", "x0", "y0", "h3", "h4", "x1", "x2", "f0",
    "q1", "q2", "x3", "x4", "c0", "y1", "r1", "r2", "y2", "f1",
    "q3", "q4", "s3", "s5", "f2", "c1", "y3", "r3", "r4", "c2", "y4", "f3",
    "q5", "q6", "s4", "f4", "h5", "h6", "c3", "x5", "y5", "r5", "r6", "x6", "y6", "c4",
    "q7", "f5", "r7", "f6", "h7", "c5", "y7", "x7", "c6", "f7", "c7",
)
TREE_BITS = (2, 1, 16, 8, 4)


def pair_coef(aa, bb, ab):
    aa, bb = jnp.maximum(aa, 0.0), jnp.maximum(bb, 0.0)
    bound = jnp.sqrt(aa) * jnp.sqrt(bb)
    return 1.0 - jnp.clip(ab, -bound, bound) / (2.0 * (aa + epsilon))


def swap(value, index, bit, axis):
    size = value.shape[axis]
    return jnp.where(
        (index & bit) != 0, pltpu.roll(value, bit, axis), pltpu.roll(value, size - bit, axis)
    )


def leaf_weights(gram):
    row = lax.broadcasted_iota(jnp.int32, gram.shape, 0)
    lane = lax.broadcasted_iota(jnp.int32, gram.shape, 1)
    weights = jnp.ones(gram.shape, jnp.float32)
    for bit in TREE_BITS:
        own = jnp.where(row == lane, gram, 0.0)
        pair = jnp.where((row ^ bit) == lane, gram, 0.0)
        far = swap(own, row, bit, 0)
        far_t = swap(own, lane, bit, 1)
        down = pair_coef(
            jnp.sum(own, axis=1, keepdims=True), jnp.sum(far, axis=1, keepdims=True),
            jnp.sum(pair, axis=1, keepdims=True),
        )
        across = pair_coef(
            jnp.sum(own, axis=0, keepdims=True), jnp.sum(far_t, axis=0, keepdims=True),
            jnp.sum(pair, axis=0, keepdims=True),
        )
        weights = weights * down
        gram = gram * down * across
        gram = gram + swap(gram, row, bit, 0)
        gram = gram + swap(gram, lane, bit, 1)
    return weights


def kernel(
    gate, up, grad, out,
    hown, hb, gb, leaf, acc, wbuf, ar, cst, obuf,
    own_sem, gx_s, gx_r, hz_s, hz_r, gz_s, gz_r, gy_s, gy_r, sib_s, sib_r, hx_s, hx_r, ar_s, ar_r, oz_s, oz_r,
):
    dp = lax.axis_index("dp")
    t = lax.axis_index("tensor")
    x, z = lax.div(dp, NZ), lax.rem(dp, NZ)
    y, core = lax.div(t, 2), lax.rem(t, 2)
    sib = y * 2 + 1 - core

    def xo(k):
        return lax.rem(x + k, NX)

    def zo(k):
        return lax.rem(z + k, NZ)

    def to(k):
        return lax.rem(t + k, NT)

    def yo(k):
        return lax.rem(y + k, 4) * 2 + core

    def at_x(k):
        return (xo(k) * NZ + z, t)

    def at_z(k):
        return (x * NZ + zo(k), t)

    def at_t(rank):
        return (dp, rank)

    def remote(src, dst, send, recv, where):
        return pltpu.make_async_remote_copy(
            src_ref=src, dst_ref=dst, send_sem=send, recv_sem=recv, device_id=where, device_id_type=MESH
        )

    sent = []

    def send(src, dst, ss, rs, where):
        copy = remote(src, dst, ss, rs, where)
        copy.start()
        sent.append(copy)

    def drain(count):
        for copy in sent[:count]:
            copy.wait_send()
        del sent[:count]

    def arrived(dst, ss, rs):
        remote(dst, dst, ss, rs, at_x(1)).wait_recv()

    def quarter(zc, yy, lo=0, n=NX, c=core):
        rows = pl.ds(pl.multiple_of(c * HR + lax.rem(y + yy, 4) * TR, TR), TR)
        return gb.at[pl.ds(lo, n), zc, rows, pl.ds(0, CS)]

    def rest(zc, lo=0, n=NX, c=core):
        return gb.at[pl.ds(lo, n), zc, pl.ds(pl.multiple_of(c * HR, HR), HR), pl.ds(CS, NB - CS)]

    barrier = pltpu.get_barrier_semaphore()
    partners = [at_x(k) for k in range(1, NX)] + [at_z(k) for k in range(1, NZ)] + [at_t(to(k)) for k in range(1, NT)]
    for where in partners:
        pl.semaphore_signal(barrier, inc=1, device_id=where, device_id_type=MESH)

    for j in range(HID // 128):
        cols = slice(128 * j, 128 * j + 128)
        v = gate[:, cols].astype(jnp.float32)
        u = up[:, cols].astype(jnp.float32)
        h = v / (1.0 + jnp.exp(-v)) * u
        hown[cols, :] = h.T.astype(jnp.bfloat16)

    pl.semaphore_wait(barrier, len(partners))

    def grad_at(p, xs):
        if p == 0:
            rows, lo, n = pl.ds(pl.multiple_of(core * HR + y * TR, TR), TR), 0, CS
        else:
            rows, lo, n = pl.ds(pl.multiple_of(core * HR, HR), HR), CS, NB - CS
        return grad.at[rows, pl.ds(pl.multiple_of(xs * NB + lo, 128), n)]

    def part_at(p, zc, lo=0, n=NX):
        return quarter(zc, 0, lo, n) if p == 0 else rest(zc, lo, n)

    own_g = []
    for p in range(2):
        for k in (1, 3, 2):
            dst = part_at(p, z, x, 1)
            send(grad_at(p, xo(k)), dst.at[0], gx_s.at[p, k], gx_r.at[p, k], at_x(k))
        own_g.append(pltpu.make_async_copy(grad_at(p, x), part_at(p, z, x, 1).at[0], own_sem.at[p]))
        own_g[p].start()

    def hown_at(zc):
        return hown.at[pl.ds(pl.multiple_of(zc * MB, 16), MB), :]

    own_h = pltpu.make_async_copy(hown_at(z), hb.at[x, z], own_sem.at[2])
    own_h.start()

    def start_hz(k):
        send(hown_at(zo(k)), hb.at[x, z], hz_s.at[k], hz_r.at[k], at_z(k))

    def to_sib(part, slot, o):
        send(part, part, sib_s.at[slot, o], sib_r.at[slot, o], at_t(sib))

    def g_z(p, i):
        o = ORDER[i]
        zc = zo(o)

        def come(way, step, lo, n):
            arrived(part_at(p, zc, lo, n), gz_s.at[way, step, p], gz_r.at[way, step, p])

        def go(way, step, lo, n):
            part = part_at(p, zc, lo, n)
            send(part, part, gz_s.at[way, step, p], gz_r.at[way, step, p], at_z(1 if way == 0 else 7))

        if o == 0:
            own_g[p].wait()
            for k in range(1, NX):
                arrived(part_at(p, z, xo(NX - k), 1).at[0], gx_s.at[p, k], gx_r.at[p, k])
            go(0, 1, 0, NX)
            go(1, 1, 0, NX)
        elif o == 4:
            come(0, 4, 0, 2)
            come(1, 4, 2, 2)
        else:
            way, step = (0, 8 - o) if o > 4 else (1, o)
            come(way, step, 0, NX)
            if step < 3:
                go(way, step + 1, 0, NX)
            else:
                go(way, 4, 2 * way, 2)
        if p == 0:
            part = quarter(zc, 0)
            send(part, part, gy_s.at[0, o], gy_r.at[0, o], at_t(yo(1)))
            send(part, part, gy_s.at[1, o], gy_r.at[1, o], at_t(yo(3)))
        to_sib(part_at(p, zc), p, o)

    def g_y(i):
        o = ORDER[i]
        zc = zo(o)
        for way in range(2):
            source = 3 if way == 0 else 1
            arrived(quarter(zc, source), gy_s.at[way, o], gy_r.at[way, o])
            part = quarter(zc, source, 2 * way, 2)
            send(part, part, gy_s.at[2 + way, o], gy_r.at[2 + way, o], at_t(yo(4 - source)))
            to_sib(quarter(zc, source), 2 + way, o)

    def g_far(i):
        o = ORDER[i]
        zc = zo(o)
        for way in range(2):
            part = quarter(zc, 2, 2 * way, 2)
            arrived(part, gy_s.at[2 + way, o], gy_r.at[2 + way, o])
            to_sib(part, 4 + way, o)

    def h_z(i):
        o = ORDER[i]
        zc = zo(o)
        if o == 0:
            own_h.wait()
        else:
            arrived(hb.at[x, zc], hz_s.at[8 - o], hz_r.at[8 - o])
        send(hb.at[x, zc], hb.at[x, zc], hx_s.at[0, o], hx_r.at[0, o], at_x(1))
        send(hb.at[x, zc], hb.at[x, zc], hx_s.at[1, o], hx_r.at[1, o], at_x(3))

    def h_x(i):
        o = ORDER[i]
        zc = zo(o)
        for way in range(2):
            xs = xo(3 if way == 0 else 1)
            arrived(hb.at[xs, zc], hx_s.at[way, o], hx_r.at[way, o])
            half = hb.at[xs, zc, pl.ds(way * (MB // 2), MB // 2), :]
            send(half, half, hx_s.at[2 + way, o], hx_r.at[2 + way, o], at_x(1 if way == 0 else 3))

    def finish(i):
        o = ORDER[i]
        zc = zo(o)
        for way in range(2):
            half = hb.at[xo(2), zc, pl.ds(way * (MB // 2), MB // 2), :]
            arrived(half, hx_s.at[2 + way, o], hx_r.at[2 + way, o])
        c = 1 - core
        parts = [quarter(zc, 0, c=c), rest(zc, c=c), quarter(zc, 3, c=c), quarter(zc, 1, c=c)]
        parts += [quarter(zc, 2, 0, 2, c=c), quarter(zc, 2, 2, 2, c=c)]
        for slot, part in enumerate(parts):
            arrived(part, sib_s.at[slot, o], sib_r.at[slot, o])

        def product(k, _):
            xx, cols = 2 * k, slice(0, NB)
            first, second = (
                jnp.dot(hb[xx + m, zc], gb[xx + m, zc, :, cols], preferred_element_type=jnp.float32) for m in range(2)
            )
            rows = pl.ds(pl.multiple_of(zc * 32 + xx * 8, 16), 16)
            for g in range(MB // 8):
                both = jnp.concatenate([first[8 * g:8 * g + 8], second[8 * g:8 * g + 8]], axis=0)
                leaf[g, rows, cols] = both.astype(jnp.bfloat16)
            return 0

        for k in range(2):
            product(k, 0)

    def all_sum(value):
        for phase, (count, me) in enumerate(((NT, t), (NX, x), (NZ, z))):
            slots = ar.at[phase]
            slots[me] = value
            for k in range(1, count):
                where = (at_t(to(k)), at_x(k), at_z(k))[phase]
                send(slots.at[me], slots.at[me], ar_s.at[phase, k], ar_r.at[phase, k], where)
            drain(54)
            for k in range(1, count):
                arrived(slots.at[lax.rem(me + count - k, count)], ar_s.at[phase, k], ar_r.at[phase, k])
            value = jnp.sum(slots[0:count], axis=0)
        return value

    stages = {
        "s": start_hz, "q": functools.partial(g_z, 0), "r": functools.partial(g_z, 1), "y": g_y, "f": g_far,
        "h": h_z, "x": h_x, "c": finish,
    }
    for step in SCHEDULE:
        stages[step[0]](int(step[1]))

    acc[...] = jnp.zeros_like(acc)

    def gram(k, _):
        total = None
        for g in range(GB):
            rows = leaf[k * GB + g]
            part = lax.dot_general(rows, rows, (((1,), (1,)), ((), ())), preferred_element_type=jnp.float32)
            total = part if total is None else total + part
        acc[...] += total
        return 0

    lax.fori_loop(0, MB // 8 // GB, gram, 0)
    index = [lax.broadcasted_iota(jnp.int32, (256, 256), axis) for axis in range(2)]
    like = jnp.where(lax.rem(index[0], 8) == lax.rem(index[1], 8), acc[...], 0.0)
    like = jnp.sum(like.reshape(32, 8, 256), axis=1)
    index = [lax.broadcasted_iota(jnp.int32, (256, 128), axis) for axis in range(2)]
    pick = jnp.where(lax.div(index[0], 8) == index[1], 1.0, 0.0).astype(jnp.float32)
    local = jnp.dot(like, pick, precision=lax.Precision.HIGHEST, preferred_element_type=jnp.float32)
    tile = local[0:8]
    for q in range(1, 4):
        tile = tile + pltpu.roll(local[8 * q:8 * q + 8], 32 * q, 1)
    tile = all_sum(tile)
    lane = lax.broadcasted_iota(jnp.int32, (8, 128), 1)
    total = [tile] + [pltpu.roll(tile, 128 - 32 * q, 1) for q in range(1, 4)]
    weights = leaf_weights(jnp.concatenate([jnp.where(lane < 32, part, 0.0) for part in total], axis=0))
    for r in range(NZ * NX):
        wbuf[r] = jnp.broadcast_to(weights[r:r + 1], (8, 128))

    for k in (4, 3, 5, 2, 6, 1, 7, 0):
        cols = pl.ds(pl.multiple_of(zo(k) * 128, 128), 128)

        def combine(g, _, k=k, cols=cols):
            totals = [jnp.zeros((8, 128), jnp.float32)] * 4
            for r in range(0, NZ * NX, 2):
                for q in range(4):
                    both = leaf[g * 4 + q, 8 * r:8 * r + 16, cols].astype(jnp.float32)
                    totals[q] = totals[q] + wbuf[r] * both[0:8] + wbuf[r + 1] * both[8:16]
            block = jnp.concatenate(totals, axis=0).astype(jnp.bfloat16)
            cst[k, pl.ds(pl.multiple_of(g * 32, 32), 32), :] = block
            return 0

        lax.fori_loop(0, MB // 32, combine, 0)
        if k:
            send(cst.at[k], obuf.at[z], oz_s.at[k], oz_r.at[k], at_z(k))
    out[pl.ds(pl.multiple_of(z * MB, 16), MB), :] = cst[0]
    for k in range(1, NZ):
        zs = zo(NZ - k)
        arrived(obuf.at[zs], oz_s.at[k], oz_r.at[k])
        out[pl.ds(pl.multiple_of(zs * MB, 16), MB), :] = obuf[zs]
    for copy in sent:
        copy.wait_send()


def body(gate_input, up_input, grad_out):
    dma = pltpu.SemaphoreType.DMA
    vmem = pl.BlockSpec(memory_space=pltpu.VMEM)
    return pl.pallas_call(
        kernel,
        out_shape=pltpu.VMEM((HID, 128), jnp.bfloat16),
        in_specs=[vmem, vmem, pl.BlockSpec(memory_space=pl.ANY)],
        out_specs=vmem,
        scratch_shapes=[
            pltpu.VMEM((HID, TOK), jnp.bfloat16),
            pltpu.VMEM((NX, NZ, MB, TOK), jnp.bfloat16),
            pltpu.VMEM((NX, NZ, TOK, NB), jnp.bfloat16),
            pltpu.VMEM((MB // 8, 256, NB), jnp.bfloat16),
            pltpu.VMEM((256, 256), jnp.float32),
            pltpu.VMEM((NZ * NX, 8, 128), jnp.float32),
            pltpu.VMEM((3, 8, 8, 128), jnp.float32),
            pltpu.VMEM((NZ, MB, 128), jnp.bfloat16),
            pltpu.VMEM((NZ, MB, 128), jnp.bfloat16),
            dma((3,)),
            dma((2, NX)), dma((2, NX)),
            dma((NZ,)), dma((NZ,)),
            dma((2, 5, 2)), dma((2, 5, 2)),
            dma((4, NZ)), dma((4, NZ)),
            dma((6, NZ)), dma((6, NZ)),
            dma((4, NZ)), dma((4, NZ)),
            dma((3, 8)), dma((3, 8)),
            dma((NZ,)), dma((NZ,)),
        ],
        compiler_params=pltpu.CompilerParams(
            collective_id=0, has_side_effects=True, vmem_limit_bytes=62 * 1024 * 1024
        ),
        cost_estimate=pl.CostEstimate(flops=3_760_000_000, bytes_accessed=5_000_000, transcendentals=460_000),
    )(gate_input, up_input, grad_out)


def solution(mesh):
    placed = (P("dp", "tensor"), P("dp", "tensor"), P("dp", None))
    return jax.shard_map(
        body, mesh=mesh, in_specs=placed, out_specs=P("tensor", "dp"), check_vma=False
    )
```
